128 devices in a mesh: ta: 32 (over z, y_lo, x), ba: 4 (over y_hi, core).
Axes of the slice: x: 4, y: 4 (y_hi: 2, y_lo: 2; y = y_hi * 2 + y_lo), z: 4, core: 2. Of those that a mesh axis runs over, the one named last changes fastest.
Arguments:
- samples: int32 [1048576, 512], P('ta', 'ba'), may hold values from -128 to 127
- input_gain: float32 [512], P('ba'), may hold values from 0.005 to 0.03
- pfb_weights: float32 [16, 1024], replicated, may hold values from -1.5 to 1.5
- chan_map: int32 [512], replicated, may hold values from 0 to 511, each once
Outputs:
- visibility: float32 [2, 512, 512, 512], P(None, ('ta', 'ba'))
The draws below stay inside these ranges and needn't reach their ends.
Inputs may be any that keep to these rules, and one draw needn't show every extreme that they name: `chan_map`: each of the 512 channel numbers appears exactly once.
All inputs are finite; a program needn't handle non-finite values.
Results may differ from the reference program's by a relative error of at most 0.0036.
Values may be sent and summed in bfloat16 or wider, within the bound.
No kernel may reach another device: no remote copies, remote signals or barrier semaphores. Data moves between devices by JAX's collectives and lax.ppermute only.
A program may use at most 128 MiB of HBM per device.

```python
import math
import jax
import jax.numpy as jnp
from jax import lax

INPUTS = 512
CHANNELS = 512
TAPS = 16
FRAME = 1024
SPECTRA = 1024
SAMPLES = 1048576


def with_ends(values, key, least, top_value):
    dims = values.shape
    place = [jax.random.randint(jax.random.fold_in(key, axis), (), 0, dims[axis]) for axis in range(len(dims))]
    values = values.at[tuple(place)].set(least)
    longest = dims.index(max(dims))
    place[longest] = (place[longest] + 1) % dims[longest]
    return values.at[tuple(place)].set(top_value)


def block_scale(stream_key, dims, split, least, largest):
    factor_of, own = 1.0, jax.random.fold_in(stream_key, 6)
    for position, parts in split:
        steps = jnp.exp(jax.random.uniform(jax.random.fold_in(own, position), (parts,), jnp.float32, least / len(split), largest / len(split)))
        factor_of = factor_of * jnp.repeat(steps, dims[position] // parts).reshape([-1 if axis == position else 1 for axis in range(len(dims))])
    return factor_of


def scatter_about(own_key, shape, deviation, reach, held_as=jnp.bfloat16):
    return jnp.clip(deviation * jax.random.normal(own_key, shape, jnp.float32), -reach, reach).astype(held_as)


def setup_inputs(seed: int = 0) -> dict:
    streams_of = jax.random.split(jax.random.key(seed), 5)
    samples = with_ends(jax.random.randint(streams_of[0], (SAMPLES, INPUTS), -128, 128), jax.random.fold_in(streams_of[0], 1), -128, 127).astype(jnp.int32)
    input_gain = jnp.clip(jnp.exp(math.log(0.03) - 1.7917595 * jax.random.uniform(streams_of[1], (INPUTS,), jnp.float32) ** block_scale(streams_of[1], (INPUTS,), ((0, 4),), -0.2, 0.2)), 0.005, 0.03)
    pfb_weights = scatter_about(streams_of[2], (TAPS, FRAME), TAPS ** -0.5, 1.5, jnp.float32)
    chan_map = jax.random.permutation(streams_of[3], CHANNELS).astype(jnp.int32)
    return {"samples": samples, "input_gain": input_gain, "pfb_weights": pfb_weights, "chan_map": chan_map}


def build_table(chan_map, frame_len):
    sample_idx = jnp.arange(frame_len, dtype=jnp.int32)
    product = sample_idx[:, None] * chan_map[None, :].astype(jnp.int32) % frame_len
    angle = product.astype(jnp.float32) * (2.0 * math.pi / frame_len)
    scale = 1.0 / math.sqrt(frame_len)
    stacked = jnp.stack([jnp.cos(angle) * scale, -jnp.sin(angle) * scale], axis=-1)
    return stacked.reshape(frame_len, -1).astype(jnp.bfloat16)

def reference(samples, input_gain, pfb_weights, chan_map):
    dft_table = build_table(chan_map, FRAME)
    block_width = min(128, INPUTS)
    pieces = []
    for start in range(0, INPUTS, block_width):
        raw = samples[:, start:start + block_width].astype(jnp.float32)
        calibrated = (raw * input_gain[None, start:start + block_width]).astype(jnp.bfloat16)
        frames = calibrated.reshape(SPECTRA, FRAME, block_width)
        extended = jnp.concatenate([jnp.zeros((TAPS - 1, FRAME, block_width), jnp.bfloat16), frames], axis=0)
        running = jnp.zeros((SPECTRA, FRAME, block_width), jnp.float32)
        for tap_index in range(TAPS):
            running = running + pfb_weights[tap_index][None, :, None] * extended[tap_index:tap_index + SPECTRA].astype(jnp.float32)
        filtered = running.astype(jnp.bfloat16)
        spectra = jnp.einsum('sni,nk->sik', filtered.astype(jnp.float32), dft_table.astype(jnp.float32))
        pieces.append(spectra.astype(jnp.bfloat16))
    spectra = jnp.concatenate(pieces, axis=1)
    group = 4 if CHANNELS % 4 == 0 else 1
    grouped = spectra.reshape(SPECTRA, INPUTS, CHANNELS // group, group, 2).transpose(2, 0, 1, 3, 4)

    def correlate(cells):
        values = cells.astype(jnp.float32)
        rotated = jnp.stack([values[..., 1], -values[..., 0]], axis=-1)
        stacked = jnp.stack([values, rotated], axis=0)
        return jnp.einsum('osicp,sjcp->ocij', stacked, values) / SPECTRA
    result = lax.map(correlate, grouped)
    return result.transpose(1, 0, 2, 3, 4).reshape(2, CHANNELS, INPUTS, INPUTS)
```

```python
import math

import jax
import jax.numpy as jnp
from jax import lax
from jax.sharding import PartitionSpec as P


def from_behind(block, axis, distance):
    devices = range(lax.axis_size(axis))
    route = [(i - distance, i) for i in devices if i - distance in devices]
    return lax.ppermute(block, axis, route)


def build_table(chan_map, frame_len):
    sample_idx = jnp.arange(frame_len, dtype=jnp.int32)
    product = chan_map[:, None] * sample_idx[None, :] % frame_len
    angle = product.astype(jnp.float32) * (2.0 * math.pi / frame_len)
    scale = 1.0 / math.sqrt(frame_len)
    stacked = jnp.stack([jnp.cos(angle) * scale, -jnp.sin(angle) * scale], axis=1)
    return stacked.reshape(-1, frame_len).astype(jnp.bfloat16)


def per_device(samples, input_gain, pfb_weights, chan_map):
    tap_count = pfb_weights.shape[0]
    frame_len = pfb_weights.shape[1]
    row_count, inputs_dev = samples.shape
    spectra_dev = row_count // frame_len
    times = lax.axis_size("ta")
    bands = lax.axis_size("ba")
    count = times * bands
    calibrated = (samples.astype(jnp.float32) * input_gain[None, :]).astype(jnp.bfloat16)
    frames = calibrated.reshape(spectra_dev, frame_len, inputs_dev)
    history = from_behind(frames[spectra_dev - (tap_count - 1) :], "ta", 1)
    weights = pfb_weights[:, :, None]
    extended = jnp.concatenate([history, frames], axis=0)
    running = jnp.zeros((spectra_dev, frame_len, inputs_dev), jnp.float32)
    for tap_index in range(tap_count):
        running = running + weights[tap_index] * extended[
            tap_index : tap_index + spectra_dev
        ].astype(jnp.float32)
    filtered = running.astype(jnp.bfloat16)
    dft_table = build_table(chan_map, frame_len)
    spectra = jnp.einsum(
        "kn,sni->ksi", dft_table, filtered, preferred_element_type=jnp.float32
    ).astype(jnp.bfloat16)
    columns = spectra.shape[0] // count
    turned = lax.all_to_all(
        spectra.reshape(count, columns, spectra_dev, inputs_dev), ("ta", "ba"), 0, 0, tiled=True
    )
    cells = turned.reshape(times, bands, columns // 2, 2, spectra_dev, inputs_dev)
    cells = cells.transpose(2, 3, 0, 4, 1, 5).reshape(
        columns // 2, 2, times * spectra_dev, bands * inputs_dev
    )
    rotated = jnp.stack([cells[:, 1], -cells[:, 0]], axis=1)
    real = jnp.einsum("cpsi,cpsj->cij", cells, cells, preferred_element_type=jnp.float32)
    imag = jnp.einsum("cpsi,cpsj->cij", rotated, cells, preferred_element_type=jnp.float32)
    return jnp.stack([real, imag]) / (times * spectra_dev)


def solution(mesh):
    placed = (P("ta", "ba"), P("ba"), P(), P())
    return jax.shard_map(
        per_device,
        mesh=mesh,
        in_specs=placed,
        out_specs=P(None, ("ta", "ba"), None, None),
        check_vma=False,
    )
```

```python
import functools
import math

import jax
import jax.numpy as jnp
import numpy as np
from jax import lax
from jax.experimental import pallas as pl
from jax.experimental.pallas import tpu as pltpu
from jax.sharding import PartitionSpec as P

LANES = 128
ROWS = 16
STEPS = 8
VMEM = 60 * 1024 * 1024
FILTER_COST = 1024


def build_table(channels, frame_len):
    turns = np.arange(channels)[:, None] * np.arange(frame_len)[None, :] % frame_len
    angle = turns * (2.0 * np.pi / frame_len)
    both = np.stack([np.cos(angle), -np.sin(angle)], axis=1) / math.sqrt(frame_len)
    return jnp.asarray(both.reshape(2 * channels, frame_len), dtype=jnp.bfloat16)


def calibrate_kernel(ahead, behind, first_ref, last_ref, gain_ref, head_ref, tail_ref):
    gain = gain_ref[...][None]
    own = last_ref.shape[0]
    head_ref[...] = (first_ref[...].astype(jnp.float32) * gain).astype(jnp.bfloat16)
    last = last_ref[own - behind :].astype(jnp.float32)
    tail_ref[...] = (last * gain).astype(jnp.bfloat16)


def calibrate_ends(frames, gain, ahead, behind):
    n_frames, frame_len, lanes = frames.shape
    part = frame_len // 4
    last = n_frames // ahead - 1
    return pl.pallas_call(
        functools.partial(calibrate_kernel, ahead, behind),
        grid=(4,),
        in_specs=[
            pl.BlockSpec((ahead, part, lanes), lambda j: (0, j, 0)),
            pl.BlockSpec((ahead, part, lanes), lambda j: (last, j, 0)),
            pl.BlockSpec((1, lanes), lambda j: (0, 0)),
        ],
        out_specs=[
            pl.BlockSpec((ahead, part, lanes), lambda j: (0, j, 0)),
            pl.BlockSpec((behind, part, lanes), lambda j: (0, j, 0)),
        ],
        out_shape=[
            jax.ShapeDtypeStruct((ahead, frame_len, lanes), jnp.bfloat16),
            jax.ShapeDtypeStruct((behind, frame_len, lanes), jnp.bfloat16),
        ],
        compiler_params=pltpu.CompilerParams(
            dimension_semantics=("arbitrary",), vmem_limit_bytes=VMEM
        ),
    )(frames, frames, gain)


def spectra_kernel(segments, taps, *refs):
    chan_ref, samples_ref, *halo_refs = refs[:-8]
    scale_ref, weight_ref, table, out_ref, part, weights, filtered, turned = refs[-8:]
    step = pl.program_id(0)
    spectra = sum(len(segment) - taps + 1 for segment in segments)
    part_rows = samples_ref.shape[1]
    columns = table.shape[0]
    pairs = spectra // 2

    @pl.when(step < STEPS)
    def _():
        weights[:, :taps] = weight_ref[...].T

        def tile(index, carry):
            row = pl.multiple_of(index * ROWS, ROWS)
            for half in range(2):
                rows = pl.ds(row + half * 8, 8)
                weight = [
                    jnp.broadcast_to(weights[rows, t : t + 1], (8, LANES)) for t in range(taps)
                ]
                base = 0
                for segment in segments:
                    count = len(segment) - taps + 1
                    sums = {}
                    for place, (source, frame, scale_row) in enumerate(segment):
                        if source == 0:
                            raw = samples_ref[frame, rows, :].astype(jnp.float32)
                            value = raw * scale_ref[scale_row : scale_row + 1, :]
                            value = value.astype(jnp.bfloat16).astype(jnp.float32)
                        else:
                            both = halo_refs[source - 1][frame, pl.ds(row, ROWS), :]
                            value = both.astype(jnp.float32)[half * 8 : half * 8 + 8]
                        for s in range(max(0, place - taps + 1), min(count, place + 1)):
                            term = value * weight[place - s]
                            sums[s] = sums[s] + term if s in sums else term
                        done = place - taps + 1
                        if done >= 0:
                            part[base + done, half * 8 : half * 8 + 8, :] = sums.pop(done)
                    base += count
            start = pl.multiple_of(step * part_rows + row, ROWS)
            for s in range(spectra):
                filtered[pl.ds(start, ROWS), s * LANES : (s + 1) * LANES] = part[s].astype(jnp.bfloat16)
            return carry

        lax.fori_loop(0, part_rows // ROWS, tile, 0)

    @pl.when(step >= STEPS)
    def _():
        pair = step - STEPS
        rhs = filtered[:, pl.ds(pl.multiple_of(pair * 2 * LANES, 2 * LANES), 2 * LANES)]
        block = 256
        for c in range(0, columns, block):
            product = jnp.dot(table[c : c + block, :], rhs, preferred_element_type=jnp.float32)
            for odd in range(2):
                turned[pl.ds(c * spectra + pair * 2 + odd, block, stride=spectra), :] = product[
                    :, odd * LANES : (odd + 1) * LANES
                ]

    @pl.when(step == STEPS + pairs - 1)
    def _():
        slots = out_ref.shape[1] // 2

        def emit(dest, carry):
            for slot in range(slots):
                rows = 2 * spectra
                first = chan_ref[dest * slots + slot] * rows
                values = turned[pl.ds(pl.multiple_of(first, rows), rows), :].astype(jnp.bfloat16)
                out_ref[dest, 2 * slot : 2 * slot + 2] = values.reshape(2, spectra, LANES)
            return carry

        lax.fori_loop(0, out_ref.shape[0], emit, 0)


def transform(segments, taps, dests, chan_map, samples, halos, scales, weights, table):
    n_frames, frame_len, lanes = samples.shape
    columns = table.shape[0]
    spectra = sum(len(segment) - taps + 1 for segment in segments)
    part_rows = frame_len // STEPS
    steps = STEPS + spectra // 2
    index = lambda j, chan: (0, jnp.minimum(j, STEPS - 1), 0)
    in_specs = [pl.BlockSpec((n_frames, part_rows, lanes), index)]
    in_specs += [pl.BlockSpec((halo.shape[0], part_rows, lanes), index) for halo in halos]
    in_specs += [
        pl.BlockSpec(scales.shape, lambda j, chan: (0, 0)),
        pl.BlockSpec((taps, part_rows), lambda j, chan: (0, jnp.minimum(j, STEPS - 1))),
        pl.BlockSpec(table.shape, lambda j, chan: (0, 0)),
    ]
    out_shape = (dests, 2 * chan_map.shape[0] // dests, spectra, lanes)
    return pl.pallas_call(
        functools.partial(spectra_kernel, segments, taps),
        grid_spec=pltpu.PrefetchScalarGridSpec(
            num_scalar_prefetch=1,
            grid=(steps,),
            in_specs=in_specs,
            out_specs=pl.BlockSpec(out_shape, lambda j, chan: (0, 0, 0, 0)),
            scratch_shapes=[
                pltpu.VMEM((spectra, ROWS, lanes), jnp.float32),
                pltpu.VMEM((part_rows, lanes), jnp.float32),
                pltpu.VMEM((frame_len, spectra * lanes), jnp.bfloat16),
                pltpu.VMEM((columns * spectra, lanes), jnp.float32),
            ],
        ),
        out_shape=jax.ShapeDtypeStruct(out_shape, jnp.bfloat16),
        compiler_params=pltpu.CompilerParams(
            dimension_semantics=("arbitrary",), vmem_limit_bytes=VMEM
        ),
        cost_estimate=pl.CostEstimate(
            flops=2 * (columns + FILTER_COST * taps) * frame_len * spectra * lanes,
            bytes_accessed=4 * n_frames * frame_len * lanes + 2 * columns * spectra * lanes,
            transcendentals=0,
        ),
    )(chan_map, samples, *halos, scales, weights, table)


def correlate_kernel(scale, *refs):
    cells_ref, *before, out_ref = refs
    times, bands, _, _, spectra, lanes = cells_ref.shape
    parts = [
        jnp.concatenate(
            [cells_ref[:, band, 0, part].reshape(times * spectra, lanes) for band in range(bands)], axis=1
        )
        for part in range(2)
    ]
    turned = [part.T for part in parts]
    dot = functools.partial(jnp.dot, preferred_element_type=jnp.float32)
    real = dot(turned[0], parts[0]) + dot(turned[1], parts[1])
    imag = dot(turned[1], parts[0]) - dot(turned[0], parts[1])
    both = real + imag
    if before:
        both = (both + before[0][0]) * (0.5 * scale)
        mirrored = both.T
        out_ref[0, 0] = both + mirrored
        out_ref[1, 0] = both - mirrored
    else:
        out_ref[0] = both


def correlate(cells, before, scale):
    times, bands, channels, _, spectra, lanes = cells.shape
    inputs = bands * lanes
    sums_spec = pl.BlockSpec((1, inputs, inputs), lambda c: (c, 0, 0))
    in_specs = [pl.BlockSpec((times, bands, 1, 2, spectra, lanes), lambda c: (0, 0, c, 0, 0, 0))]
    if before is None:
        more, out_shape, out_spec = [], (channels, inputs, inputs), sums_spec
    else:
        more, out_shape = [before], (2, channels, inputs, inputs)
        out_spec = pl.BlockSpec((2, 1, inputs, inputs), lambda c: (0, c, 0, 0))
        in_specs.append(sums_spec)
    return pl.pallas_call(
        functools.partial(correlate_kernel, scale),
        grid=(channels,),
        in_specs=in_specs,
        out_specs=out_spec,
        out_shape=jax.ShapeDtypeStruct(out_shape, jnp.float32),
        compiler_params=pltpu.CompilerParams(
            dimension_semantics=("arbitrary",), vmem_limit_bytes=VMEM
        ),
        cost_estimate=pl.CostEstimate(
            flops=8 * channels * inputs * inputs * times * spectra,
            bytes_accessed=2 * cells.size + 8 * channels * inputs * inputs,
            transcendentals=0,
        ),
    )(cells, *more)


def per_device(samples, input_gain, pfb_weights, chan_map):
    taps, frame_len = pfb_weights.shape
    row_count, lanes = samples.shape
    own = row_count // frame_len
    times = lax.axis_size("ta")
    bands = lax.axis_size("ba")
    dests = times * bands
    ahead = taps // 2
    behind = taps - 1 - ahead
    frames = samples.reshape(own, frame_len, lanes)

    head, tail = calibrate_ends(frames, input_gain[None, :], ahead, behind)
    history = lax.ppermute(tail, "ta", [(i, i + 1) for i in range(times - 1)])
    future = lax.ppermute(head, "ta", [(i, (i - 1) % times) for i in range(times)])
    is_last = lax.axis_index("ta") == times - 1
    scales = jnp.stack([input_gain, jnp.where(is_last, 0.0, input_gain)])
    table = build_table(chan_map.shape[0], frame_len)

    inner = [[(0, f, 0) for f in range(1, own)]]
    outer = [
        [(1, f, 0) for f in range(behind)] + [(0, f, 0) for f in range(taps)],
        [(0, f, 1) for f in range(own - taps + 1, own)] + [(2, f, 0) for f in range(ahead)],
    ]

    def turn(spectra):
        got = lax.all_to_all(spectra, ("ta", "ba"), 0, 0, tiled=True)
        _, columns, count, _ = got.shape
        return got.reshape(times, bands, columns // 2, 2, count, lanes)

    shared = (scales, pfb_weights, table)
    first = turn(transform(inner, taps, dests, chan_map, frames, [], *shared))
    second = turn(transform(outer, taps, dests, chan_map, frames, [history, future], *shared))
    sums = correlate(first, None, 1.0)
    return correlate(second, sums, 1.0 / (times * own))


def solution(mesh):
    placed = (P("ta", "ba"), P("ba"), P(), P())
    return jax.shard_map(
        per_device,
        mesh=mesh,
        in_specs=placed,
        out_specs=P(None, ("ta", "ba"), None, None),
        check_vma=False,
    )
```

```python
import functools
import math

import jax
import jax.numpy as jnp
import numpy as np
from jax import lax
from jax.experimental import pallas as pl
from jax.experimental.pallas import tpu as pltpu
from jax.sharding import PartitionSpec as P

LANES = 128
ROWS = 16
STEPS = 8
CALIBRATE_STEPS = 2
VMEM = 60 * 1024 * 1024
FILTER_COST = 1024


def build_table(channels, frame_len):
    turns = np.arange(channels)[:, None] * np.arange(frame_len)[None, :] % frame_len
    angle = turns * (2.0 * np.pi / frame_len)
    both = np.stack([np.cos(angle), -np.sin(angle)], axis=1) / math.sqrt(frame_len)
    return jnp.asarray(both.reshape(2 * channels, frame_len), dtype=jnp.bfloat16)


def calibrate_kernel(frames_ref, gain_ref, out_ref):
    values = frames_ref[...].astype(jnp.float32)
    out_ref[...] = (values * gain_ref[...][None]).astype(jnp.bfloat16)


def calibrate(frames, gain, place, count):
    _, frame_len, lanes = frames.shape
    part = frame_len // CALIBRATE_STEPS
    return pl.pallas_call(
        calibrate_kernel,
        grid=(CALIBRATE_STEPS,),
        in_specs=[
            pl.BlockSpec((count, part, lanes), lambda j: (place, j, 0)),
            pl.BlockSpec((1, lanes), lambda j: (0, 0)),
        ],
        out_specs=pl.BlockSpec((count, part, lanes), lambda j: (0, j, 0)),
        out_shape=jax.ShapeDtypeStruct((count, frame_len, lanes), jnp.bfloat16),
        compiler_params=pltpu.CompilerParams(
            dimension_semantics=("arbitrary",), vmem_limit_bytes=VMEM
        ),
    )(frames, gain)


def filter_rows(segments, taps, row, samples_ref, halo_refs, scale_ref, weights, before, emit):
    both = pl.ds(row, ROWS)
    for half in range(2):
        rows = pl.ds(row + half * 8, 8)
        weight = [jnp.broadcast_to(weights[rows, t : t + 1], (8, LANES)) for t in range(taps)]
        base = 0
        for segment in segments:
            count = len(segment) - taps + 1
            sums = {s: before(base + s, rows) for s in range(count)} if before else {}
            for place, entry in enumerate(segment):
                if entry is not None:
                    source, frame, scale_row = entry
                    if source == 0:
                        raw = samples_ref[frame, rows, :].astype(jnp.float32)
                        value = raw * scale_ref[scale_row : scale_row + 1, :]
                        value = value.astype(jnp.bfloat16).astype(jnp.float32)
                    else:
                        value = halo_refs[source - 1][frame, both, :].astype(jnp.float32)
                        value = value[half * 8 : half * 8 + 8]
                    for s in range(max(0, place - taps + 1), min(count, place + 1)):
                        term = value * weight[place - s]
                        sums[s] = sums[s] + term if s in sums else term
                done = place - taps + 1
                if done >= 0:
                    emit(base + done, half, sums.pop(done))
            base += count


def partial_kernel(segments, taps, samples_ref, halo_ref, scale_ref, weight_ref, out_ref, weights):
    weights[:, :taps] = weight_ref[...].T

    def tile(index, carry):
        row = pl.multiple_of(index * ROWS, ROWS)

        def emit(s, half, total):
            out_ref[s, pl.ds(row + half * 8, 8), :] = total

        filter_rows(
            segments, taps, row, samples_ref, [halo_ref], scale_ref, weights, None, emit
        )
        return carry

    lax.fori_loop(0, out_ref.shape[1] // ROWS, tile, 0)


def filter_part(segments, taps, samples, halo, scales, weights):
    n_frames, frame_len, lanes = samples.shape
    spectra = sum(len(segment) - taps + 1 for segment in segments)
    part_rows = frame_len // STEPS
    index = lambda j: (0, j, 0)
    return pl.pallas_call(
        functools.partial(partial_kernel, segments, taps),
        grid=(STEPS,),
        in_specs=[
            pl.BlockSpec((n_frames, part_rows, lanes), index),
            pl.BlockSpec((halo.shape[0], part_rows, lanes), index),
            pl.BlockSpec(scales.shape, lambda j: (0, 0)),
            pl.BlockSpec((taps, part_rows), lambda j: (0, j)),
        ],
        out_specs=pl.BlockSpec((spectra, part_rows, lanes), index),
        out_shape=jax.ShapeDtypeStruct((spectra, frame_len, lanes), jnp.float32),
        scratch_shapes=[pltpu.VMEM((part_rows, lanes), jnp.float32)],
        compiler_params=pltpu.CompilerParams(
            dimension_semantics=("arbitrary",), vmem_limit_bytes=VMEM
        ),
        cost_estimate=pl.CostEstimate(
            flops=2 * FILTER_COST * taps * frame_len * spectra * lanes,
            bytes_accessed=4 * (n_frames + spectra) * frame_len * lanes,
            transcendentals=0,
        ),
    )(samples, halo, scales, weights)


def spectra_kernel(segments, taps, chan_ref, source_ref, *refs):
    *halo_refs, scale_ref, weight_ref, table, out_ref, weights, filtered, turned = refs
    step = pl.program_id(0)
    spectra = sum(len(segment) - taps + 1 for segment in segments)
    part_rows = source_ref.shape[1]
    columns = table.shape[0]
    pairs = spectra // 2

    @pl.when(step < STEPS)
    def _():
        weights[:, :taps] = weight_ref[...].T

        def tile(index, carry):
            row = pl.multiple_of(index * ROWS, ROWS)
            start = pl.multiple_of(step * part_rows + row, ROWS)

            def emit(s, half, total):
                filtered[pl.ds(start + half * 8, 8), s * LANES : (s + 1) * LANES] = total

            before = (lambda s, rows: source_ref[s, rows, :]) if halo_refs else None
            filter_rows(
                segments, taps, row, source_ref, halo_refs, scale_ref, weights, before, emit
            )
            return carry

        lax.fori_loop(0, part_rows // ROWS, tile, 0)

    @pl.when(step >= STEPS)
    def _():
        pair = step - STEPS
        rhs = filtered[:, pl.ds(pl.multiple_of(pair * 2 * LANES, 2 * LANES), 2 * LANES)]
        rhs = rhs.astype(jnp.bfloat16)
        block = 256
        for c in range(0, columns, block):
            product = jnp.dot(table[c : c + block, :], rhs, preferred_element_type=jnp.float32)
            for odd in range(2):
                turned[pl.ds(c * spectra + pair * 2 + odd, block, stride=spectra), :] = product[
                    :, odd * LANES : (odd + 1) * LANES
                ]

    @pl.when(step == STEPS + pairs - 1)
    def _():
        slots = out_ref.shape[1] // 2
        group = 2

        def emit(index, carry):
            rows = 2 * spectra
            places = [(index * group + here, slot) for here in range(group) for slot in range(slots)]
            values = []
            for dest, slot in places:
                first = chan_ref[dest * slots + slot] * rows
                values.append(turned[pl.ds(pl.multiple_of(first, rows), rows), :].astype(jnp.bfloat16))
            for (dest, slot), value in zip(places, values):
                out_ref[dest, 2 * slot : 2 * slot + 2] = value.reshape(2, spectra, LANES)
            return carry

        lax.fori_loop(0, out_ref.shape[0] // group, emit, 0)


def transform(segments, taps, dests, chan_map, source, halos, scales, weights, table):
    n_frames, frame_len, lanes = source.shape
    columns = table.shape[0]
    spectra = sum(len(segment) - taps + 1 for segment in segments)
    part_rows = frame_len // STEPS
    steps = STEPS + spectra // 2
    index = lambda j, chan: (0, jnp.minimum(j, STEPS - 1), 0)
    in_specs = [pl.BlockSpec((n_frames, part_rows, lanes), index)]
    in_specs += [pl.BlockSpec((halo.shape[0], part_rows, lanes), index) for halo in halos]
    in_specs += [
        pl.BlockSpec(scales.shape, lambda j, chan: (0, 0)),
        pl.BlockSpec((taps, part_rows), lambda j, chan: (0, jnp.minimum(j, STEPS - 1))),
        pl.BlockSpec(table.shape, lambda j, chan: (0, 0)),
    ]
    out_shape = (dests, 2 * chan_map.shape[0] // dests, spectra, lanes)
    return pl.pallas_call(
        functools.partial(spectra_kernel, segments, taps),
        grid_spec=pltpu.PrefetchScalarGridSpec(
            num_scalar_prefetch=1,
            grid=(steps,),
            in_specs=in_specs,
            out_specs=pl.BlockSpec(out_shape, lambda j, chan: (0, 0, 0, 0)),
            scratch_shapes=[
                pltpu.VMEM((part_rows, lanes), jnp.float32),
                pltpu.VMEM((frame_len, spectra * lanes), jnp.float32),
                pltpu.VMEM((columns * spectra, lanes), jnp.float32),
            ],
        ),
        out_shape=jax.ShapeDtypeStruct(out_shape, jnp.bfloat16),
        compiler_params=pltpu.CompilerParams(
            dimension_semantics=("arbitrary",), vmem_limit_bytes=VMEM
        ),
        cost_estimate=pl.CostEstimate(
            flops=2 * (columns + (0 if halos else FILTER_COST * taps)) * frame_len * spectra * lanes,
            bytes_accessed=4 * n_frames * frame_len * lanes + 2 * columns * spectra * lanes,
            transcendentals=0,
        ),
    )(chan_map, source, *halos, scales, weights, table)


def correlate_kernel(scale, *refs):
    cells_ref, *before, out_ref = refs
    times, bands, _, _, spectra, lanes = cells_ref.shape
    parts = [
        jnp.concatenate(
            [cells_ref[:, band, 0, part].reshape(times * spectra, lanes) for band in range(bands)], axis=1
        )
        for part in range(2)
    ]
    turned = [part.T for part in parts]
    dot = functools.partial(jnp.dot, preferred_element_type=jnp.float32)
    real = dot(turned[0], parts[0]) + dot(turned[1], parts[1])
    imag = dot(turned[1], parts[0]) - dot(turned[0], parts[1])
    both = real + imag
    if before:
        both = (both + before[0][0]) * (0.5 * scale)
        mirrored = both.T
        out_ref[0, 0] = both + mirrored
        out_ref[1, 0] = both - mirrored
    else:
        out_ref[0] = both


def correlate(cells, before, scale):
    times, bands, channels, _, spectra, lanes = cells.shape
    inputs = bands * lanes
    sums_spec = pl.BlockSpec((1, inputs, inputs), lambda c: (c, 0, 0))
    in_specs = [pl.BlockSpec((times, bands, 1, 2, spectra, lanes), lambda c: (0, 0, c, 0, 0, 0))]
    if before is None:
        more, out_shape, out_spec = [], (channels, inputs, inputs), sums_spec
    else:
        more, out_shape = [before], (2, channels, inputs, inputs)
        out_spec = pl.BlockSpec((2, 1, inputs, inputs), lambda c: (0, c, 0, 0))
        in_specs.append(sums_spec)
    return pl.pallas_call(
        functools.partial(correlate_kernel, scale),
        grid=(channels,),
        in_specs=in_specs,
        out_specs=out_spec,
        out_shape=jax.ShapeDtypeStruct(out_shape, jnp.float32),
        compiler_params=pltpu.CompilerParams(
            dimension_semantics=("arbitrary",), vmem_limit_bytes=VMEM
        ),
        cost_estimate=pl.CostEstimate(
            flops=8 * channels * inputs * inputs * times * spectra,
            bytes_accessed=2 * cells.size + 8 * channels * inputs * inputs,
            transcendentals=0,
        ),
    )(cells, *more)


def per_device(samples, input_gain, pfb_weights, chan_map):
    taps, frame_len = pfb_weights.shape
    row_count, lanes = samples.shape
    own = row_count // frame_len
    times = lax.axis_size("ta")
    bands = lax.axis_size("ba")
    dests = times * bands
    behind = taps // 2
    ahead = taps - 1 - behind
    frames = samples.reshape(own, frame_len, lanes)

    gain = input_gain[None, :]
    head = calibrate(frames, gain, 0, ahead)
    tail = calibrate(frames, gain, own // behind - 1, behind)
    future = lax.ppermute(head, "ta", [(i, (i - 1) % times) for i in range(times)])
    history = lax.ppermute(tail, "ta", [(i, i + 1) for i in range(times - 1)])
    is_last = lax.axis_index("ta") == times - 1
    scales = jnp.stack([input_gain, jnp.where(is_last, 0.0, input_gain)])
    table = build_table(chan_map.shape[0], frame_len)

    inner = [[(0, f, 0) for f in range(1, own)]]
    early = [
        [(1, f, 0) for f in range(behind)] + [(0, f, 0) for f in range(taps)],
        [(0, f, 1) for f in range(own - taps + 1, own)] + [None] * ahead,
    ]
    late = [[None] * (behind + taps), [None] * (taps - 1) + [(1, f, 0) for f in range(ahead)]]

    def turn(spectra):
        got = lax.all_to_all(spectra, ("ta", "ba"), 0, 0, tiled=True)
        _, columns, count, _ = got.shape
        return got.reshape(times, bands, columns // 2, 2, count, lanes)

    shared = (scales, pfb_weights, table)
    first = turn(transform(inner, taps, dests, chan_map, frames, [], *shared))
    part = filter_part(early, taps, frames, history, scales, pfb_weights)
    second = turn(transform(late, taps, dests, chan_map, part, [future], *shared))
    sums = correlate(first, None, 1.0)
    return correlate(second, sums, 1.0 / (times * own))


def solution(mesh):
    placed = (P("ta", "ba"), P("ba"), P(), P())
    return jax.shard_map(
        per_device,
        mesh=mesh,
        in_specs=placed,
        out_specs=P(None, ("ta", "ba"), None, None),
        check_vma=False,
    )
```

```python
import functools
import math

import jax
import jax.numpy as jnp
import numpy as np
from jax import lax
from jax.experimental import pallas as pl
from jax.experimental.pallas import tpu as pltpu
from jax.sharding import PartitionSpec as P

LANES = 128
ROWS = 16
STEPS = 8
CALIBRATE_STEPS = 2
VMEM = 60 * 1024 * 1024
FILTER_COST = 1024


def build_table(channels, frame_len):
    turns = np.arange(channels)[:, None] * np.arange(frame_len)[None, :] % frame_len
    angle = turns * (2.0 * np.pi / frame_len)
    both = np.stack([np.cos(angle), -np.sin(angle)], axis=1) / math.sqrt(frame_len)
    return jnp.asarray(both.reshape(2 * channels, frame_len), dtype=jnp.bfloat16)


def calibrate_kernel(frames_ref, gain_ref, out_ref):
    values = frames_ref[...].astype(jnp.float32)
    out_ref[...] = (values * gain_ref[...][None]).astype(jnp.bfloat16)


def calibrate(frames, gain, place, count):
    _, frame_len, lanes = frames.shape
    part = frame_len // CALIBRATE_STEPS
    return pl.pallas_call(
        calibrate_kernel,
        grid=(CALIBRATE_STEPS,),
        in_specs=[
            pl.BlockSpec((count, part, lanes), lambda j: (place, j, 0)),
            pl.BlockSpec((1, lanes), lambda j: (0, 0)),
        ],
        out_specs=pl.BlockSpec((count, part, lanes), lambda j: (0, j, 0)),
        out_shape=jax.ShapeDtypeStruct((count, frame_len, lanes), jnp.bfloat16),
        compiler_params=pltpu.CompilerParams(
            dimension_semantics=("arbitrary",), vmem_limit_bytes=VMEM
        ),
    )(frames, gain)


def filter_rows(segments, taps, row, samples_ref, halo_refs, scale_ref, weights, before, emit):
    both = pl.ds(row, ROWS)
    for half in range(2):
        rows = pl.ds(row + half * 8, 8)
        weight = [jnp.broadcast_to(weights[rows, t : t + 1], (8, LANES)) for t in range(taps)]
        base = 0
        for segment in segments:
            count = len(segment) - taps + 1
            sums = {s: before(base + s, rows) for s in range(count)} if before else {}
            for place, entry in enumerate(segment):
                if entry is not None:
                    source, frame, scale_row = entry
                    if source == 0:
                        raw = samples_ref[frame, rows, :].astype(jnp.float32)
                        value = raw * scale_ref[scale_row : scale_row + 1, :]
                        value = value.astype(jnp.bfloat16).astype(jnp.float32)
                    else:
                        value = halo_refs[source - 1][frame, both, :].astype(jnp.float32)
                        value = value[half * 8 : half * 8 + 8]
                    for s in range(max(0, place - taps + 1), min(count, place + 1)):
                        term = value * weight[place - s]
                        sums[s] = sums[s] + term if s in sums else term
                done = place - taps + 1
                if done >= 0:
                    emit(base + done, half, sums.pop(done))
            base += count


def partial_kernel(segments, taps, samples_ref, halo_ref, scale_ref, weight_ref, out_ref, weights):
    weights[:, :taps] = weight_ref[...].T

    def tile(index, carry):
        row = pl.multiple_of(index * ROWS, ROWS)

        def emit(s, half, total):
            out_ref[s, pl.ds(row + half * 8, 8), :] = total

        filter_rows(
            segments, taps, row, samples_ref, [halo_ref], scale_ref, weights, None, emit
        )
        return carry

    lax.fori_loop(0, out_ref.shape[1] // ROWS, tile, 0)


def filter_part(segments, taps, samples, halo, scales, weights):
    n_frames, frame_len, lanes = samples.shape
    spectra = sum(len(segment) - taps + 1 for segment in segments)
    part_rows = frame_len // STEPS
    index = lambda j: (0, j, 0)
    return pl.pallas_call(
        functools.partial(partial_kernel, segments, taps),
        grid=(STEPS,),
        in_specs=[
            pl.BlockSpec((n_frames, part_rows, lanes), index),
            pl.BlockSpec((halo.shape[0], part_rows, lanes), index),
            pl.BlockSpec(scales.shape, lambda j: (0, 0)),
            pl.BlockSpec((taps, part_rows), lambda j: (0, j)),
        ],
        out_specs=pl.BlockSpec((spectra, part_rows, lanes), index),
        out_shape=jax.ShapeDtypeStruct((spectra, frame_len, lanes), jnp.float32),
        scratch_shapes=[pltpu.VMEM((part_rows, lanes), jnp.float32)],
        compiler_params=pltpu.CompilerParams(
            dimension_semantics=("arbitrary",), vmem_limit_bytes=VMEM
        ),
        cost_estimate=pl.CostEstimate(
            flops=2 * FILTER_COST * taps * frame_len * spectra * lanes,
            bytes_accessed=4 * (n_frames + spectra) * frame_len * lanes,
            transcendentals=0,
        ),
    )(samples, halo, scales, weights)


def spectra_kernel(segments, taps, chan_ref, source_ref, *refs):
    *halo_refs, scale_ref, weight_ref, table, out_ref, weights, filtered, turned = refs
    step = pl.program_id(0)
    spectra = sum(len(segment) - taps + 1 for segment in segments)
    part_rows = source_ref.shape[1]
    columns = table.shape[0]
    pairs = spectra // 2

    @pl.when(step < STEPS)
    def _():
        weights[:, :taps] = weight_ref[...].T

        def tile(index, carry):
            row = pl.multiple_of(index * ROWS, ROWS)
            start = pl.multiple_of(step * part_rows + row, ROWS)

            def emit(s, half, total):
                filtered[pl.ds(start + half * 8, 8), s * LANES : (s + 1) * LANES] = total

            before = (lambda s, rows: source_ref[s, rows, :]) if halo_refs else None
            filter_rows(
                segments, taps, row, source_ref, halo_refs, scale_ref, weights, before, emit
            )
            return carry

        lax.fori_loop(0, part_rows // ROWS, tile, 0)

    @pl.when(step >= STEPS)
    def _():
        pair = step - STEPS
        rhs = filtered[:, pl.ds(pl.multiple_of(pair * 2 * LANES, 2 * LANES), 2 * LANES)]
        rhs = rhs.astype(jnp.bfloat16)
        block = 256
        for c in range(0, columns, block):
            product = jnp.dot(table[c : c + block, :], rhs, preferred_element_type=jnp.float32)
            for odd in range(2):
                turned[pl.ds(c * spectra + pair * 2 + odd, block, stride=spectra), :] = product[
                    :, odd * LANES : (odd + 1) * LANES
                ]

    @pl.when(step == STEPS + pairs - 1)
    def _():
        slots = out_ref.shape[1] // 2
        group = 2

        def emit(index, carry):
            rows = 2 * spectra
            places = [(index * group + here, slot) for here in range(group) for slot in range(slots)]
            values = []
            for dest, slot in places:
                first = chan_ref[dest * slots + slot] * rows
                values.append(turned[pl.ds(pl.multiple_of(first, rows), rows), :].astype(jnp.bfloat16))
            for (dest, slot), value in zip(places, values):
                out_ref[dest, 2 * slot : 2 * slot + 2] = value.reshape(2, spectra, LANES)
            return carry

        lax.fori_loop(0, out_ref.shape[0] // group, emit, 0)


def transform(segments, taps, dests, chan_map, source, halos, scales, weights, table):
    n_frames, frame_len, lanes = source.shape
    columns = table.shape[0]
    spectra = sum(len(segment) - taps + 1 for segment in segments)
    part_rows = frame_len // STEPS
    steps = STEPS + spectra // 2
    index = lambda j, chan: (0, jnp.minimum(j, STEPS - 1), 0)
    in_specs = [pl.BlockSpec((n_frames, part_rows, lanes), index)]
    in_specs += [pl.BlockSpec((halo.shape[0], part_rows, lanes), index) for halo in halos]
    in_specs += [
        pl.BlockSpec(scales.shape, lambda j, chan: (0, 0)),
        pl.BlockSpec((taps, part_rows), lambda j, chan: (0, jnp.minimum(j, STEPS - 1))),
        pl.BlockSpec(table.shape, lambda j, chan: (0, 0)),
    ]
    out_shape = (dests, 2 * chan_map.shape[0] // dests, spectra, lanes)
    return pl.pallas_call(
        functools.partial(spectra_kernel, segments, taps),
        grid_spec=pltpu.PrefetchScalarGridSpec(
            num_scalar_prefetch=1,
            grid=(steps,),
            in_specs=in_specs,
            out_specs=pl.BlockSpec(out_shape, lambda j, chan: (0, 0, 0, 0)),
            scratch_shapes=[
                pltpu.VMEM((part_rows, lanes), jnp.float32),
                pltpu.VMEM((frame_len, spectra * lanes), jnp.float32),
                pltpu.VMEM((columns * spectra, lanes), jnp.float32),
            ],
        ),
        out_shape=jax.ShapeDtypeStruct(out_shape, jnp.bfloat16),
        compiler_params=pltpu.CompilerParams(
            dimension_semantics=("arbitrary",), vmem_limit_bytes=VMEM
        ),
        cost_estimate=pl.CostEstimate(
            flops=2 * (columns + (0 if halos else FILTER_COST * taps)) * frame_len * spectra * lanes,
            bytes_accessed=4 * n_frames * frame_len * lanes + 2 * columns * spectra * lanes,
            transcendentals=0,
        ),
    )(chan_map, source, *halos, scales, weights, table)


def sums_of(cells):
    times, bands, _, spectra, lanes = cells.shape
    parts = [
        jnp.concatenate(
            [cells[:, band, part].reshape(times * spectra, lanes) for band in range(bands)], axis=1
        )
        for part in range(2)
    ]
    turned = [part.T for part in parts]
    dot = functools.partial(jnp.dot, preferred_element_type=jnp.float32)
    real = dot(turned[0], parts[0]) + dot(turned[1], parts[1])
    return real + (dot(turned[1], parts[0]) - dot(turned[0], parts[1]))


def sums_kernel(cells_ref, out_ref):
    out_ref[0] = sums_of(cells_ref.at[:, :, 0])


def correlate_kernel(scale, cells_hbm, before_hbm, out_hbm, cells, before, out, cells_sem, before_sem, out_sem):
    channels = cells.shape[0]
    reads = [
        (
            pltpu.make_async_copy(cells_hbm.at[:, :, c], cells.at[c], cells_sem.at[c]),
            pltpu.make_async_copy(before_hbm.at[c], before.at[c], before_sem.at[c]),
        )
        for c in range(channels)
    ]
    for read_cells, read_before in reads:
        read_cells.start()
        read_before.start()
    writes = []
    for c, (read_cells, read_before) in enumerate(reads):
        read_cells.wait()
        both = sums_of(cells.at[c])
        read_before.wait()
        both = (both + before[c]) * (0.5 * scale)
        mirrored = both.T
        out[c, 0] = both + mirrored
        out[c, 1] = both - mirrored
        writes.append(pltpu.make_async_copy(out.at[c], out_hbm.at[:, c], out_sem.at[c]))
        writes[-1].start()
    for write in writes:
        write.wait()


def correlate(cells, before, scale):
    times, bands, channels, _, spectra, lanes = cells.shape
    inputs = bands * lanes
    params = dict(vmem_limit_bytes=VMEM)
    cost = pl.CostEstimate(
        flops=8 * channels * inputs * inputs * times * spectra,
        bytes_accessed=2 * cells.size + 8 * channels * inputs * inputs,
        transcendentals=0,
    )
    if before is None:
        return pl.pallas_call(
            sums_kernel,
            grid=(channels,),
            in_specs=[
                pl.BlockSpec((times, bands, 1, 2, spectra, lanes), lambda c: (0, 0, c, 0, 0, 0))
            ],
            out_specs=pl.BlockSpec((1, inputs, inputs), lambda c: (c, 0, 0)),
            out_shape=jax.ShapeDtypeStruct((channels, inputs, inputs), jnp.float32),
            compiler_params=pltpu.CompilerParams(dimension_semantics=("arbitrary",), **params),
            cost_estimate=cost,
        )(cells)
    return pl.pallas_call(
        functools.partial(correlate_kernel, scale),
        in_specs=[pl.BlockSpec(memory_space=pl.ANY)] * 2,
        out_specs=pl.BlockSpec(memory_space=pl.ANY),
        out_shape=jax.ShapeDtypeStruct((2, channels, inputs, inputs), jnp.float32),
        scratch_shapes=[
            pltpu.VMEM((channels, times, bands, 2, spectra, lanes), cells.dtype),
            pltpu.VMEM((channels, inputs, inputs), jnp.float32),
            pltpu.VMEM((channels, 2, inputs, inputs), jnp.float32),
            pltpu.SemaphoreType.DMA((channels,)),
            pltpu.SemaphoreType.DMA((channels,)),
            pltpu.SemaphoreType.DMA((channels,)),
        ],
        compiler_params=pltpu.CompilerParams(**params),
        cost_estimate=cost,
    )(cells, before)


def per_device(samples, input_gain, pfb_weights, chan_map):
    taps, frame_len = pfb_weights.shape
    row_count, lanes = samples.shape
    own = row_count // frame_len
    times = lax.axis_size("ta")
    bands = lax.axis_size("ba")
    dests = times * bands
    behind = taps // 2
    ahead = taps - 1 - behind
    frames = samples.reshape(own, frame_len, lanes)

    gain = input_gain[None, :]
    head = calibrate(frames, gain, 0, ahead)
    tail = calibrate(frames, gain, own // behind - 1, behind)
    future = lax.ppermute(head, "ta", [(i, (i - 1) % times) for i in range(times)])
    history = lax.ppermute(tail, "ta", [(i, i + 1) for i in range(times - 1)])
    is_last = lax.axis_index("ta") == times - 1
    scales = jnp.stack([input_gain, jnp.where(is_last, 0.0, input_gain)])
    table = build_table(chan_map.shape[0], frame_len)

    inner = [[(0, f, 0) for f in range(1, own)]]
    early = [
        [(1, f, 0) for f in range(behind)] + [(0, f, 0) for f in range(taps)],
        [(0, f, 1) for f in range(own - taps + 1, own)] + [None] * ahead,
    ]
    late = [[None] * (behind + taps), [None] * (taps - 1) + [(1, f, 0) for f in range(ahead)]]

    def turn(spectra):
        got = lax.all_to_all(spectra, ("ta", "ba"), 0, 0, tiled=True)
        _, columns, count, _ = got.shape
        return got.reshape(times, bands, columns // 2, 2, count, lanes)

    shared = (scales, pfb_weights, table)
    first = turn(transform(inner, taps, dests, chan_map, frames, [], *shared))
    part = filter_part(early, taps, frames, history, scales, pfb_weights)
    second = turn(transform(late, taps, dests, chan_map, part, [future], *shared))
    sums = correlate(first, None, 1.0)
    return correlate(second, sums, 1.0 / (times * own))


def solution(mesh):
    placed = (P("ta", "ba"), P("ba"), P(), P())
    return jax.shard_map(
        per_device,
        mesh=mesh,
        in_specs=placed,
        out_specs=P(None, ("ta", "ba"), None, None),
        check_vma=False,
    )
```

```python
import functools
import math

import jax
import jax.numpy as jnp
import numpy as np
from jax import lax
from jax.experimental import pallas as pl
from jax.experimental.pallas import tpu as pltpu
from jax.sharding import PartitionSpec as P

LANES = 128
ROWS = 16
STEPS = 8
CALIBRATE_STEPS = 2
VMEM = 48 * 1024 * 1024
FILTER_COST = 1024


def build_table(channels, frame_len):
    turns = np.arange(channels)[:, None] * np.arange(frame_len)[None, :] % frame_len
    angle = turns * (2.0 * np.pi / frame_len)
    both = np.stack([np.cos(angle), -np.sin(angle)], axis=1) / math.sqrt(frame_len)
    return jnp.asarray(both.reshape(2 * channels, frame_len), dtype=jnp.bfloat16)


def calibrate_kernel(frames_ref, gain_ref, out_ref):
    values = frames_ref[...].astype(jnp.float32)
    out_ref[...] = (values * gain_ref[...][None]).astype(jnp.bfloat16)


def calibrate(frames, gain, place, count):
    _, frame_len, lanes = frames.shape
    part = frame_len // CALIBRATE_STEPS
    return pl.pallas_call(
        calibrate_kernel,
        grid=(CALIBRATE_STEPS,),
        in_specs=[
            pl.BlockSpec((count, part, lanes), lambda j: (place, j, 0)),
            pl.BlockSpec((1, lanes), lambda j: (0, 0)),
        ],
        out_specs=pl.BlockSpec((count, part, lanes), lambda j: (0, j, 0)),
        out_shape=jax.ShapeDtypeStruct((count, frame_len, lanes), jnp.bfloat16),
        compiler_params=pltpu.CompilerParams(
            dimension_semantics=("arbitrary",), vmem_limit_bytes=VMEM
        ),
    )(frames, gain)


def filter_rows(segments, taps, row, samples_ref, halo_refs, scale_ref, weights, before, emit):
    both = pl.ds(row, ROWS)
    for half in range(2):
        rows = pl.ds(row + half * 8, 8)
        weight = [jnp.broadcast_to(weights[rows, t : t + 1], (8, LANES)) for t in range(taps)]
        base = 0
        for segment in segments:
            count = len(segment) - taps + 1
            sums = {s: before(base + s, rows) for s in range(count)} if before else {}
            for place, entry in enumerate(segment):
                if entry is not None:
                    source, frame, scale_row = entry
                    if source == 0:
                        raw = samples_ref[frame, rows, :].astype(jnp.float32)
                        value = raw * scale_ref[scale_row : scale_row + 1, :]
                        value = value.astype(jnp.bfloat16).astype(jnp.float32)
                    else:
                        value = halo_refs[source - 1][frame, both, :].astype(jnp.float32)
                        value = value[half * 8 : half * 8 + 8]
                    for s in range(max(0, place - taps + 1), min(count, place + 1)):
                        term = value * weight[place - s]
                        sums[s] = sums[s] + term if s in sums else term
                done = place - taps + 1
                if done >= 0:
                    emit(base + done, half, sums.pop(done))
            base += count


def partial_kernel(segments, taps, samples_ref, halo_ref, scale_ref, weight_ref, out_ref, weights):
    weights[:, :taps] = weight_ref[...].T

    def tile(index, carry):
        row = pl.multiple_of(index * ROWS, ROWS)

        def emit(s, half, total):
            out_ref[s, pl.ds(row + half * 8, 8), :] = total

        filter_rows(
            segments, taps, row, samples_ref, [halo_ref], scale_ref, weights, None, emit
        )
        return carry

    lax.fori_loop(0, out_ref.shape[1] // ROWS, tile, 0)


def filter_part(segments, taps, samples, halo, scales, weights):
    n_frames, frame_len, lanes = samples.shape
    spectra = sum(len(segment) - taps + 1 for segment in segments)
    part_rows = frame_len // STEPS
    index = lambda j: (0, j, 0)
    return pl.pallas_call(
        functools.partial(partial_kernel, segments, taps),
        grid=(STEPS,),
        in_specs=[
            pl.BlockSpec((n_frames, part_rows, lanes), index),
            pl.BlockSpec((halo.shape[0], part_rows, lanes), index),
            pl.BlockSpec(scales.shape, lambda j: (0, 0)),
            pl.BlockSpec((taps, part_rows), lambda j: (0, j)),
        ],
        out_specs=pl.BlockSpec((spectra, part_rows, lanes), index),
        out_shape=jax.ShapeDtypeStruct((spectra, frame_len, lanes), jnp.float32),
        scratch_shapes=[pltpu.VMEM((part_rows, lanes), jnp.float32)],
        compiler_params=pltpu.CompilerParams(
            dimension_semantics=("arbitrary",), vmem_limit_bytes=VMEM
        ),
        cost_estimate=pl.CostEstimate(
            flops=2 * FILTER_COST * taps * frame_len * spectra * lanes,
            bytes_accessed=4 * (n_frames + spectra) * frame_len * lanes,
            transcendentals=0,
        ),
    )(samples, halo, scales, weights)


def spectra_kernel(segments, taps, chan_ref, source_ref, *refs):
    *halo_refs, scale_ref, weight_ref, table, out_ref, weights, filtered, turned = refs
    step = pl.program_id(0)
    spectra = sum(len(segment) - taps + 1 for segment in segments)
    part_rows = source_ref.shape[1]
    columns = table.shape[0]
    pairs = spectra // 2

    @pl.when(step < STEPS)
    def _():
        weights[:, :taps] = weight_ref[...].T

        def tile(index, carry):
            row = pl.multiple_of(index * ROWS, ROWS)
            start = pl.multiple_of(step * part_rows + row, ROWS)

            def emit(s, half, total):
                filtered[pl.ds(start + half * 8, 8), s * LANES : (s + 1) * LANES] = total

            before = (lambda s, rows: source_ref[s, rows, :]) if halo_refs else None
            filter_rows(
                segments, taps, row, source_ref, halo_refs, scale_ref, weights, before, emit
            )
            return carry

        lax.fori_loop(0, part_rows // ROWS, tile, 0)

    @pl.when(step >= STEPS)
    def _():
        pair = step - STEPS
        rhs = filtered[:, pl.ds(pl.multiple_of(pair * 2 * LANES, 2 * LANES), 2 * LANES)]
        rhs = rhs.astype(jnp.bfloat16)
        block = 256
        for c in range(0, columns, block):
            product = jnp.dot(table[c : c + block, :], rhs, preferred_element_type=jnp.float32)
            for odd in range(2):
                turned[pl.ds(c * spectra + pair * 2 + odd, block, stride=spectra), :] = product[
                    :, odd * LANES : (odd + 1) * LANES
                ]

    @pl.when(step == STEPS + pairs - 1)
    def _():
        slots = out_ref.shape[1] // 2
        group = 2

        def emit(index, carry):
            rows = 2 * spectra
            places = [(index * group + here, slot) for here in range(group) for slot in range(slots)]
            values = []
            for dest, slot in places:
                first = chan_ref[dest * slots + slot] * rows
                values.append(turned[pl.ds(pl.multiple_of(first, rows), rows), :].astype(jnp.bfloat16))
            for (dest, slot), value in zip(places, values):
                out_ref[dest, 2 * slot : 2 * slot + 2] = value.reshape(2, spectra, LANES)
            return carry

        lax.fori_loop(0, out_ref.shape[0] // group, emit, 0)


def transform(segments, taps, dests, chan_map, source, halos, scales, weights, table):
    n_frames, frame_len, lanes = source.shape
    columns = table.shape[0]
    spectra = sum(len(segment) - taps + 1 for segment in segments)
    part_rows = frame_len // STEPS
    steps = STEPS + spectra // 2
    index = lambda j, chan: (0, jnp.minimum(j, STEPS - 1), 0)
    in_specs = [pl.BlockSpec((n_frames, part_rows, lanes), index)]
    in_specs += [pl.BlockSpec((halo.shape[0], part_rows, lanes), index) for halo in halos]
    in_specs += [
        pl.BlockSpec(scales.shape, lambda j, chan: (0, 0)),
        pl.BlockSpec((taps, part_rows), lambda j, chan: (0, jnp.minimum(j, STEPS - 1))),
        pl.BlockSpec(table.shape, lambda j, chan: (0, 0)),
    ]
    out_shape = (dests, 2 * chan_map.shape[0] // dests, spectra, lanes)
    return pl.pallas_call(
        functools.partial(spectra_kernel, segments, taps),
        grid_spec=pltpu.PrefetchScalarGridSpec(
            num_scalar_prefetch=1,
            grid=(steps,),
            in_specs=in_specs,
            out_specs=pl.BlockSpec(out_shape, lambda j, chan: (0, 0, 0, 0)),
            scratch_shapes=[
                pltpu.VMEM((part_rows, lanes), jnp.float32),
                pltpu.VMEM((frame_len, spectra * lanes), jnp.float32),
                pltpu.VMEM((columns * spectra, lanes), jnp.float32),
            ],
        ),
        out_shape=jax.ShapeDtypeStruct(out_shape, jnp.bfloat16),
        compiler_params=pltpu.CompilerParams(
            dimension_semantics=("arbitrary",), vmem_limit_bytes=VMEM
        ),
        cost_estimate=pl.CostEstimate(
            flops=2 * (columns + (0 if halos else FILTER_COST * taps)) * frame_len * spectra * lanes,
            bytes_accessed=4 * n_frames * frame_len * lanes + 2 * columns * spectra * lanes,
            transcendentals=0,
        ),
    )(chan_map, source, *halos, scales, weights, table)


def sums_of(cells):
    times, bands, _, spectra, lanes = cells.shape
    parts = [
        jnp.concatenate(
            [cells[:, band, part].reshape(times * spectra, lanes) for band in range(bands)], axis=1
        )
        for part in range(2)
    ]
    turned = [part.T for part in parts]
    dot = functools.partial(jnp.dot, preferred_element_type=jnp.float32)
    real = dot(turned[0], parts[0]) + dot(turned[1], parts[1])
    return real + (dot(turned[1], parts[0]) - dot(turned[0], parts[1]))


def sums_kernel(cells_ref, out_ref):
    out_ref[0] = sums_of(cells_ref.at[:, :, 0])


def correlate_kernel(scale, cells_hbm, before_hbm, out_hbm, cells, before, out, cells_sem, before_sem, out_sem):
    channels = cells.shape[0]
    reads = [
        (
            pltpu.make_async_copy(cells_hbm.at[:, :, c], cells.at[c], cells_sem.at[c]),
            pltpu.make_async_copy(before_hbm.at[c], before.at[c], before_sem.at[c]),
        )
        for c in range(channels)
    ]
    for read_cells, read_before in reads:
        read_cells.start()
        read_before.start()
    writes = []
    for c, (read_cells, read_before) in enumerate(reads):
        read_cells.wait()
        both = sums_of(cells.at[c])
        read_before.wait()
        both = (both + before[c]) * (0.5 * scale)
        mirrored = both.T
        out[c, 0] = both + mirrored
        out[c, 1] = both - mirrored
        writes.append(pltpu.make_async_copy(out.at[c], out_hbm.at[:, c], out_sem.at[c]))
        writes[-1].start()
    for write in writes:
        write.wait()


def correlate(cells, before, scale):
    times, bands, channels, _, spectra, lanes = cells.shape
    inputs = bands * lanes
    params = dict(vmem_limit_bytes=VMEM)
    cost = pl.CostEstimate(
        flops=8 * channels * inputs * inputs * times * spectra,
        bytes_accessed=2 * cells.size + 8 * channels * inputs * inputs,
        transcendentals=0,
    )
    if before is None:
        return pl.pallas_call(
            sums_kernel,
            grid=(channels,),
            in_specs=[
                pl.BlockSpec((times, bands, 1, 2, spectra, lanes), lambda c: (0, 0, c, 0, 0, 0))
            ],
            out_specs=pl.BlockSpec((1, inputs, inputs), lambda c: (c, 0, 0)),
            out_shape=jax.ShapeDtypeStruct((channels, inputs, inputs), jnp.float32),
            compiler_params=pltpu.CompilerParams(dimension_semantics=("arbitrary",), **params),
            cost_estimate=cost,
        )(cells)
    return pl.pallas_call(
        functools.partial(correlate_kernel, scale),
        in_specs=[pl.BlockSpec(memory_space=pl.ANY)] * 2,
        out_specs=pl.BlockSpec(memory_space=pl.ANY),
        out_shape=jax.ShapeDtypeStruct((2, channels, inputs, inputs), jnp.float32),
        scratch_shapes=[
            pltpu.VMEM((channels, times, bands, 2, spectra, lanes), cells.dtype),
            pltpu.VMEM((channels, inputs, inputs), jnp.float32),
            pltpu.VMEM((channels, 2, inputs, inputs), jnp.float32),
            pltpu.SemaphoreType.DMA((channels,)),
            pltpu.SemaphoreType.DMA((channels,)),
            pltpu.SemaphoreType.DMA((channels,)),
        ],
        compiler_params=pltpu.CompilerParams(**params),
        cost_estimate=cost,
    )(cells, before)


def per_device(samples, input_gain, pfb_weights, chan_map):
    taps, frame_len = pfb_weights.shape
    row_count, lanes = samples.shape
    own = row_count // frame_len
    times = lax.axis_size("ta")
    bands = lax.axis_size("ba")
    dests = times * bands
    behind = taps // 2
    ahead = taps - 1 - behind
    frames = samples.reshape(own, frame_len, lanes)

    gain = input_gain[None, :]
    head = calibrate(frames, gain, 0, ahead)
    tail = calibrate(frames, gain, own // behind - 1, behind)
    future = lax.ppermute(head, "ta", [(i, (i - 1) % times) for i in range(times)])
    history = lax.ppermute(tail, "ta", [(i, i + 1) for i in range(times - 1)])
    is_last = lax.axis_index("ta") == times - 1
    scales = jnp.stack([input_gain, jnp.where(is_last, 0.0, input_gain)])
    table = build_table(chan_map.shape[0], frame_len)

    inner = [[(0, f, 0) for f in range(1, own)]]
    early = [
        [(1, f, 0) for f in range(behind)] + [(0, f, 0) for f in range(taps)],
        [(0, f, 1) for f in range(own - taps + 1, own)] + [None] * ahead,
    ]
    late = [[None] * (behind + taps), [None] * (taps - 1) + [(1, f, 0) for f in range(ahead)]]

    def turn(spectra):
        got = lax.all_to_all(spectra, ("ta", "ba"), 0, 0, tiled=True)
        _, columns, count, _ = got.shape
        return got.reshape(times, bands, columns // 2, 2, count, lanes)

    shared = (scales, pfb_weights, table)
    first = turn(transform(inner, taps, dests, chan_map, frames, [], *shared))
    part = filter_part(early, taps, frames, history, scales, pfb_weights)
    second = turn(transform(late, taps, dests, chan_map, part, [future], *shared))
    sums = correlate(first, None, 1.0)
    return correlate(second, sums, 1.0 / (times * own))


def solution(mesh):
    placed = (P("ta", "ba"), P("ba"), P(), P())
    return jax.shard_map(
        per_device,
        mesh=mesh,
        in_specs=placed,
        out_specs=P(None, ("ta", "ba"), None, None),
        check_vma=False,
    )
```
